512 devices in a mesh: seq: 32 (over x, y), state: 16 (over z, core).
Axes of the slice: x: 4, y: 8, z: 8, core: 2. Of those that a mesh axis runs over, the one named last changes fastest.
Arguments:
- inputs: bfloat16 [16384, 2048], P('seq', 'state'), may hold values from -6 to 6
- out_grad: bfloat16 [16384, 2048], P('seq', 'state'), may hold values from -6 to 6
- in_proj: bfloat16 [2048, 2048], P('state'), may hold values from -0.125 to 0.125
- out_proj: bfloat16 [2048, 2048], P(None, 'state'), may hold values from -0.125 to 0.125
- rates: float32 [2048], P('state'), may hold values from 1.2207031e-05 to 0.03
- time_step: float32 [16384], P('seq'), may hold values from 0.5 to 65536, as said below
Outputs:
- grad_inputs: bfloat16 [16384, 2048], P('seq', 'state')
- grad_in_proj: float32 [2048, 2048], P('state')
- grad_out_proj: float32 [2048, 2048], P(None, 'state')
- grad_rates: float32 [2048], P('state')
The draws below stay inside these ranges and needn't reach their ends.
Inputs may be any that keep to these rules, and one draw needn't show every extreme that they name: `time_step`: positive time steps.
All inputs are finite; a program needn't handle non-finite values.
Results may differ from the reference program's by a relative error of at most 0.017.
Values may be sent and summed in bfloat16 or wider, within the bound.
No kernel may reach another device: no remote copies, remote signals or barrier semaphores. Data moves between devices by JAX's collectives and lax.ppermute only.
A program may use at most 64 MiB of HBM per device.

```python
import math
import jax
import jax.numpy as jnp
from jax import lax

H = 2048
N = 2048
SPAN_LENGTH = 16384
N_STATE = 16


def draw_time_step(key, part):
    first = jax.random.fold_in(key, 11)
    second = jax.random.fold_in(key, 12)
    final_segment = jax.random.fold_in(key, 13)
    starting_index = jnp.exp(jax.random.uniform(first, (SPAN_LENGTH,), jnp.float32, jnp.log(0.5), jnp.log(2.0)))
    location_indices = jax.random.randint(second, (8,), 0, SPAN_LENGTH)
    clustered_batches = jax.random.uniform(final_segment, (8,), jnp.float32, 0.125, 0.35) * (10.0 * SPAN_LENGTH)
    return starting_index.at[location_indices].set(clustered_batches)


def block_levels(key, dims, shards, low, largest):
    level, own = 1.0, jax.random.fold_in(key, 6)
    for dim, shards_of in shards:
        draws = jnp.exp(jax.random.uniform(jax.random.fold_in(own, dim), (shards_of,), jnp.float32, low / len(shards), largest / len(shards)))
        level = level * jnp.repeat(draws, dims[dim] // shards_of).reshape([-1 if axis == dim else 1 for axis in range(len(dims))])
    return level


def noise(key, shape, spread, bound, shards=(), dtype=jnp.bfloat16):
    array = spread * jax.random.normal(key, shape, jnp.float32)
    if shards:
        array = array * block_levels(key, shape, shards, -0.22, 0.18)
    return jnp.clip(array, -bound, bound).astype(dtype)


def setup_inputs(seed: int = 0) -> dict:
    key_list = jax.random.split(jax.random.key(seed), 7)
    inputs = noise(key_list[0], (SPAN_LENGTH, H), 1.0, 6.0, ((0, 32), (1, 16)))
    out_grad = noise(key_list[1], (SPAN_LENGTH, H), 1.0, 6.0, ((0, 32), (1, 16)))
    in_proj = noise(key_list[2], (N, H), H ** -0.5, 0.125, ((0, 16),))
    out_proj = noise(key_list[3], (H, N), N ** -0.5, 0.125, ((1, 16),))
    rates = jnp.clip(jnp.exp(math.log(0.03) - 7.8069405 * jax.random.uniform(key_list[4], (N,), jnp.float32) ** block_levels(key_list[4], (N,), ((0, 16),), -0.2, 0.2)), 1.220703143189894e-05, 0.03)
    time_step = draw_time_step(jax.random.fold_in(key_list[6], 71), 0)
    return dict(inputs=inputs, out_grad=out_grad, in_proj=in_proj, out_proj=out_proj, rates=rates, time_step=time_step)


def combine(earlier, later):
    return (earlier[0] * later[0], later[0] * earlier[1] + later[1])


def reference(inputs, out_grad, in_proj, out_proj, rates, time_step):
    decay = jnp.exp(-time_step[:, None] * rates[None, :])
    drive = lax.dot_general(inputs, in_proj, (((1,), (1,)), ((), ())), preferred_element_type=jnp.float32)
    adjoint_in = jnp.dot(out_grad, out_proj, preferred_element_type=jnp.float32)
    states = lax.associative_scan(combine, (decay, drive), axis=0)[1]
    coefs = jnp.concatenate([decay[1:], jnp.zeros((1, decay.shape[1]), jnp.float32)], axis=0)
    flipped = lax.associative_scan(combine, (coefs[::-1], adjoint_in[::-1]), axis=0)[1]
    adjoint = flipped[::-1]
    states_half = states.astype(jnp.bfloat16)
    adjoint_half = adjoint.astype(jnp.bfloat16)
    before = jnp.concatenate([jnp.zeros((1, states.shape[1]), jnp.float32), states[:-1]], axis=0)
    grad_rates = -jnp.sum(time_step[:, None] * decay * adjoint * before, axis=0)
    grad_in_proj = lax.dot_general(adjoint_half, inputs, (((0,), (0,)), ((), ())), preferred_element_type=jnp.float32)
    grad_out_proj = lax.dot_general(out_grad, states_half, (((0,), (0,)), ((), ())), preferred_element_type=jnp.float32)
    width = N // N_STATE

    def add_block(index, total):
        start = (index * width).astype(jnp.int32)
        part_adj = lax.dynamic_slice_in_dim(adjoint_half, start, width, 1)
        part_proj = lax.dynamic_slice_in_dim(in_proj, start, width, 0)
        partial_sum = jnp.dot(part_adj, part_proj, preferred_element_type=jnp.float32)
        return total + partial_sum.astype(jnp.bfloat16).astype(jnp.float32)

    total = lax.fori_loop(0, N_STATE, add_block, jnp.zeros((adjoint.shape[0], in_proj.shape[1]), jnp.float32))
    return total.astype(jnp.bfloat16), grad_in_proj, grad_out_proj, grad_rates
```

```python
import jax
import jax.numpy as jnp
from jax import lax
from jax.experimental import pallas as pl
from jax.experimental.pallas import tpu as pltpu
from jax.sharding import PartitionSpec as P

F32 = jnp.float32
BF16 = jnp.bfloat16
LANES = 128
ROWS = 8
LIMIT = 48 * 1024 * 1024


def call(kernel, out_shape, scratch=(), cost=None, **specs):
    return pl.pallas_call(
        kernel,
        out_shape=out_shape,
        **specs,
        scratch_shapes=list(scratch),
        compiler_params=pltpu.CompilerParams(vmem_limit_bytes=LIMIT),
        cost_estimate=cost,
    )


def estimate(flops, nbytes):
    return pl.CostEstimate(flops=flops, bytes_accessed=nbytes, transcendentals=0)


def strand(step, tokens):
    return pl.ds(step, ROWS, tokens // ROWS)


def by_rows(values, last_first):
    rows, total = [None] * ROWS, jnp.ones_like(values[0:1])
    for k in reversed(range(ROWS)) if last_first else range(ROWS):
        rows[k] = total
        total = total * values[k : k + 1]
    return jnp.concatenate(rows, axis=0), total


def decays_kernel(
    dt_ref, rates_ref, dec_ref, cum_ref, rem_ref, out_cum, out_rem, w_ad, w_a, w_b, bd_ref
):
    tokens = dt_ref.shape[0]
    steps = tokens // ROWS
    dec_ref[...] = jnp.exp(-dt_ref[...] * rates_ref[...])
    total = dec_ref[strand(0, tokens), :]
    cum_ref[strand(0, tokens), :] = total
    for j in range(1, steps):
        total = total * dec_ref[strand(j, tokens), :]
        cum_ref[strand(j, tokens), :] = total
    ahead = jnp.ones_like(total)
    for j in reversed(range(steps)):
        rem_ref[strand(j, tokens), :] = ahead
        ahead = ahead * dec_ref[strand(j, tokens), :]
    before, whole = by_rows(total, False)
    after, _ = by_rows(total, True)
    for j in range(steps):
        at = strand(j, tokens)
        out_cum[at, :] = cum_ref[at, :] * before
        out_rem[at, :] = rem_ref[at, :] * after
    w_ad[...] = dt_ref[...] * dec_ref[...]
    w_a[...] = dt_ref[...] * out_cum[...]
    w_b[...] = w_ad[...] * out_rem[...]
    bd_ref[0:1, :] = whole
    bd_ref[1:2, :] = whole * jnp.sum(jnp.broadcast_to(dt_ref[...], dec_ref.shape), axis=0, keepdims=True)


def scans_kernel(
    g_ref, inp_ref, outp_ref, dec_ref, cum_ref, rem_ref, w_ad, w_a, w_b, bd_ref,
    st_ref, ad_ref, carry_ref, drive, adj_in,
):
    blocks, both, _ = g_ref.shape
    tokens = both // 2
    steps = tokens // ROWS
    x = jnp.concatenate([g_ref[k, :tokens, :] for k in range(blocks)], axis=1)
    drive[...] = lax.dot_general(x, inp_ref[...], (((1,), (1,)), ((), ())), preferred_element_type=F32)
    y = jnp.concatenate([g_ref[k, tokens:, :] for k in range(blocks)], axis=1)
    adj_in[...] = jnp.dot(y, outp_ref[...], preferred_element_type=F32)
    state = drive[strand(0, tokens), :]
    st_ref[strand(0, tokens), :] = state
    for j in range(1, steps):
        at = strand(j, tokens)
        state = dec_ref[at, :] * state + drive[at, :]
        st_ref[at, :] = state
    adjoint = adj_in[strand(steps - 1, tokens), :]
    ad_ref[strand(steps - 1, tokens), :] = adjoint
    for j in reversed(range(steps - 1)):
        at = strand(j, tokens)
        adjoint = dec_ref[strand(j + 1, tokens), :] * adjoint + adj_in[at, :]
        ad_ref[at, :] = adjoint
    span = cum_ref[strand(steps - 1, tokens), :]
    first = dec_ref[strand(0, tokens), :] * adjoint
    rows, entering = [], jnp.zeros((1, LANES), F32)
    for k in range(ROWS):
        rows.append(entering)
        entering = span[k : k + 1] * entering + state[k : k + 1]
    into = jnp.concatenate(rows, axis=0)
    rows, leaving = [None] * ROWS, jnp.zeros((1, LANES), F32)
    for k in reversed(range(ROWS)):
        rows[k] = leaving
        leaving = span[k : k + 1] * leaving + first[k : k + 1]
    back = jnp.concatenate(rows, axis=0)
    sums = [jnp.zeros((ROWS, LANES), F32)] * 3
    previous = into
    for j in range(steps):
        at = strand(j, tokens)
        state = st_ref[at, :] + cum_ref[at, :] * into
        adjoint = ad_ref[at, :] + rem_ref[at, :] * back
        st_ref[at, :] = state
        ad_ref[at, :] = adjoint
        sums = [
            sums[0] + w_ad[at, :] * adjoint * previous,
            sums[1] + w_a[at, :] * adjoint,
            sums[2] + w_b[at, :] * previous,
        ]
        previous = state
    sums = [jnp.sum(s, axis=0, keepdims=True) for s in sums]
    block = jnp.concatenate(
        [bd_ref[0:1, :], entering, leaving, *sums, bd_ref[1:2, :], jnp.zeros((1, LANES), F32)], axis=0
    )
    for s in range(carry_ref.shape[0]):
        carry_ref[s] = block


def products_kernel(
    me_ref, carry_ref, g_ref, st_ref, ad_ref, cum_ref, rem_ref,
    half_ref, grads_ref, rates_ref, into, back,
):
    devices = carry_ref.shape[0]
    blocks, both, _ = g_ref.shape
    tokens = both // 2
    entering = jnp.zeros((1, LANES), F32)
    for s in range(devices):
        into[s : s + 1, :] = entering
        entering = carry_ref[s, 0:1, :] * entering + carry_ref[s, 1:2, :]
    leaving = jnp.zeros((1, LANES), F32)
    total = jnp.zeros((1, LANES), F32)
    for s in reversed(range(devices)):
        back[s : s + 1, :] = leaving
        here = into[s : s + 1, :]
        total = total + (
            carry_ref[s, 3:4, :]
            + carry_ref[s, 4:5, :] * here
            + leaving * (carry_ref[s, 5:6, :] + carry_ref[s, 6:7, :] * here)
        )
        leaving = carry_ref[s, 0:1, :] * leaving + carry_ref[s, 2:3, :]
    rates_ref[...] = -total
    me = me_ref[0]
    adjoint = (ad_ref[...] + rem_ref[...] * back[pl.ds(me, 1), :]).astype(BF16)
    half_ref[...] = adjoint
    state = (st_ref[...] + cum_ref[...] * into[pl.ds(me, 1), :]).astype(BF16)
    half = LANES // 2
    pair = 2 * LANES
    for k in range(0, blocks, 2):
        x = jnp.concatenate([g_ref[k, :tokens, :], g_ref[k + 1, :tokens, :]], axis=1)
        y = jnp.concatenate([g_ref[k, tokens:, :], g_ref[k + 1, tokens:, :]], axis=1)
        gi = lax.dot_general(adjoint, x, (((0,), (0,)), ((), ())), preferred_element_type=F32)
        go = lax.dot_general(state, y, (((0,), (0,)), ((), ())), preferred_element_type=F32)
        for q in range(2):
            lanes = slice(q * LANES, (q + 1) * LANES)
            a = gi[:, lanes].astype(BF16)
            b = go[:, lanes].T.astype(BF16)
            for r in range(2):
                rows = slice(r * half, (r + 1) * half)
                grads_ref[2 * (k + q) + r, :half, :] = a[rows]
                grads_ref[2 * (k + q) + r, half:, :] = b[rows]


def sum_kernel(parts_ref, out_ref):
    total = parts_ref[0].astype(F32)
    for s in range(1, parts_ref.shape[0]):
        total = total + parts_ref[s].astype(F32)
    total = total.astype(BF16)
    for s in range(out_ref.shape[0]):
        out_ref[s] = total


def finish_kernel(parts_ref, gi_ref, go_ref):
    half = LANES // 2
    for k in range(parts_ref.shape[0] // 2):
        for r in range(2):
            rows = slice(r * half, (r + 1) * half)
            gi_ref[rows, k * LANES : (k + 1) * LANES] = parts_ref[2 * k + r, :half, :].astype(F32)
            go_ref[k * LANES + r * half : k * LANES + (r + 1) * half, :] = parts_ref[2 * k + r, half:, :].astype(F32)


def inputs_kernel(half_ref, col_ref, out_ref):
    blocks = half_ref.shape[0]
    a = jnp.concatenate([half_ref[k] for k in range(blocks)], axis=1)
    w = jnp.concatenate([col_ref[k] for k in range(blocks)], axis=0)
    out_ref[...] = jnp.dot(a, w, preferred_element_type=F32).astype(BF16)


def on_device(inputs, out_grad, in_proj, out_proj, rates, time_step):
    tokens = inputs.shape[0]
    features = in_proj.shape[1]
    blocks = lax.axis_size("state")
    devices = lax.axis_size("seq")
    sds = jax.ShapeDtypeStruct
    seen = sds((tokens, LANES), F32)
    gathered = lax.all_gather(jnp.concatenate([inputs, out_grad], axis=0), "state", axis=0)
    columns = lax.all_to_all(
        jnp.moveaxis(in_proj.reshape(LANES, blocks, LANES), 1, 0), "state", 0, 0, tiled=True
    )
    dec, near, far, cum, rem, *weights = call(
        decays_kernel,
        (seen,) * 8 + (sds((2, LANES), F32),),
    )(time_step[:, None], rates[None, :])
    states, adjoints, carry = call(
        scans_kernel,
        (seen, seen, sds((devices, ROWS, LANES), F32)),
        scratch=[pltpu.VMEM((tokens, LANES), F32)] * 2,
        cost=estimate(4 * tokens * features * LANES, 7 << 20),
    )(gathered, in_proj, out_proj, dec, near, far, *weights)
    carry = lax.all_to_all(carry, "seq", 0, 0, tiled=True)
    me = lax.axis_index("seq").astype(jnp.int32).reshape(1)
    vmem = pl.BlockSpec(memory_space=pltpu.VMEM)
    half, grads, grad_rates = call(
        products_kernel,
        (
            sds((tokens, LANES), BF16),
            sds((devices, features * 2 // devices, LANES), BF16),
            sds((1, LANES), F32),
        ),
        in_specs=[pl.BlockSpec(memory_space=pltpu.SMEM)] + [vmem] * 6,
        scratch=[pltpu.VMEM((devices, LANES), F32)] * 2,
        cost=estimate(4 * tokens * features * LANES, 7 << 20),
    )(me, carry, gathered, states, adjoints, cum, rem)
    half_all = lax.all_gather(half, "state", axis=0)
    grads = lax.all_to_all(grads, "seq", 0, 0, tiled=True)
    grads = call(sum_kernel, sds(grads.shape, BF16))(grads)
    grads = lax.all_to_all(grads, "seq", 0, 0, tiled=True)
    grad_inputs = call(
        inputs_kernel,
        sds((tokens, LANES), BF16),
        cost=estimate(2 * tokens * features * LANES, 3 << 20),
    )(half_all, columns)
    grad_in, grad_out = call(
        finish_kernel, (sds((LANES, features), F32), sds((features, LANES), F32))
    )(grads)
    return grad_inputs, grad_in, grad_out, grad_rates[0]


def solution(mesh):
    placed = (
        P("seq", "state"),
        P("seq", "state"),
        P("state", None),
        P(None, "state"),
        P("state"),
        P("seq"),
    )
    return jax.shard_map(
        on_device,
        mesh=mesh,
        in_specs=placed,
        out_specs=(P("seq", "state"), P("state", None), P(None, "state"), P("state")),
        check_vma=False,
    )
```

```python
import jax
import jax.numpy as jnp
from jax import lax
from jax.experimental import pallas as pl
from jax.experimental.pallas import tpu as pltpu
from jax.sharding import PartitionSpec as P

F32 = jnp.float32
BF16 = jnp.bfloat16
LANES = 128
ROWS = 8
INNER = 8
LIMIT = 32 * 1024 * 1024
VMEM = pl.BlockSpec(memory_space=pltpu.VMEM)
SMEM = pl.BlockSpec(memory_space=pltpu.SMEM)
HBM = pl.BlockSpec(memory_space=pltpu.HBM)
SCANS = 48 * 1024 * 1024
PRODS = 48 * 1024 * 1024
FINISH = 48 * 1024 * 1024
ANY = pl.BlockSpec(memory_space=pl.ANY)
DECAY, NEAR, FAR, BOTH, FIRST, SECOND, CUM, REM, KINDS = range(9)


def call(kernel, out_shape, scratch=(), cost=None, limit=LIMIT, **specs):
    return pl.pallas_call(
        kernel,
        out_shape=out_shape,
        **specs,
        scratch_shapes=list(scratch),
        compiler_params=pltpu.CompilerParams(vmem_limit_bytes=limit),
        cost_estimate=cost,
    )


def estimate(flops, nbytes):
    return pl.CostEstimate(flops=flops, bytes_accessed=nbytes, transcendentals=0)


def strand(step, tokens):
    return pl.ds(step, ROWS, tokens // ROWS)


def by_rows(values, last_first):
    rows, total = [None] * ROWS, jnp.ones_like(values[0:1])
    for k in reversed(range(ROWS)) if last_first else range(ROWS):
        rows[k] = total
        total = total * values[k : k + 1]
    return jnp.concatenate(rows, axis=0), total


def fetch(source, which, held, sems):
    copies = [
        pltpu.make_async_copy(source.at[w], held.at[n], sems.at[n]) for n, w in enumerate(which)
    ]
    for copy in copies:
        copy.start()
    return copies


def decays_kernel(dt_ref, rates_ref, col_ref, d_ref, ends_ref):
    tokens = dt_ref.shape[0]
    steps = tokens // ROWS
    dec_ref, near_ref, far_ref = d_ref.at[DECAY], d_ref.at[NEAR], d_ref.at[FAR]
    cum_ref, rem_ref = d_ref.at[CUM], d_ref.at[REM]
    dec_ref[...] = jnp.exp(-dt_ref[...] * rates_ref[...])
    total = dec_ref[strand(0, tokens), :]
    near_ref[strand(0, tokens), :] = total
    for j in range(1, steps):
        total = total * dec_ref[strand(j, tokens), :]
        near_ref[strand(j, tokens), :] = total
    ahead = jnp.ones_like(total)
    for j in reversed(range(steps)):
        far_ref[strand(j, tokens), :] = ahead
        ahead = ahead * dec_ref[strand(j, tokens), :]
    before, whole = by_rows(total, False)
    after, _ = by_rows(total, True)
    for j in range(steps):
        at = strand(j, tokens)
        cum_ref[at, :] = near_ref[at, :] * before
        rem_ref[at, :] = far_ref[at, :] * after
    d_ref[BOTH] = dt_ref[...] * dec_ref[...]
    d_ref[FIRST] = dt_ref[...] * cum_ref[...]
    d_ref[SECOND] = dt_ref[...] * dec_ref[...] * rem_ref[...]
    ends_ref[:ROWS, :] = total
    summed = jnp.sum(jnp.broadcast_to(dt_ref[...], dec_ref.shape), axis=0, keepdims=True)
    ends_ref[ROWS:, :] = jnp.concatenate(
        [whole, whole * summed, jnp.zeros((ROWS - 2, LANES), F32)], axis=0
    )


PARTS = 4


def join_kernel(a_ref, b_ref, out_ref, held, sems):
    rows = a_ref.shape[0]
    stays = [pl.ds(n * rows, rows) for n in range(2)]
    comes = [
        pltpu.make_async_copy(ref, held.at[at], sems.at[n])
        for n, (ref, at) in enumerate(zip((a_ref, b_ref), stays))
    ]
    goes = [
        pltpu.make_async_copy(held.at[at], out_ref.at[at], sems.at[2 + n])
        for n, at in enumerate(stays)
    ]
    for copy in comes:
        copy.start()
    for come, go in zip(comes, goes):
        come.wait()
        go.start()
    for copy in goes:
        copy.wait()


def fetch_parts(g_ref, held, sems):
    step = g_ref.shape[0] // PARTS
    copies = [
        pltpu.make_async_copy(
            g_ref.at[pl.ds(c * step, step)], held.at[pl.ds(c * step, step)], sems.at[c]
        )
        for c in range(PARTS)
    ]
    for copy in copies:
        copy.start()
    return copies, step


def scans_kernel(
    me_ref, g_ref, in_ref, out_ref, d_ref, ends_ref,
    st_ref, ad_ref, carry_ref, drive, adj_in, held, sems, kept, kept_sems, inp_ref, outp_ref, w_sems,
):
    weights = [
        pltpu.make_async_copy(in_ref, inp_ref, w_sems.at[0]),
        pltpu.make_async_copy(out_ref, outp_ref, w_sems.at[1]),
    ]
    for copy in weights:
        copy.start()
    copies, step = fetch_parts(g_ref, held, sems)
    others = fetch(d_ref, (DECAY, NEAR, FAR, BOTH, FIRST, SECOND), kept, kept_sems)
    tokens = st_ref.shape[0]
    steps = tokens // ROWS
    for copy in weights:
        copy.wait()
    x, y = 0.0, 0.0
    for c, copy in enumerate(copies):
        copy.wait()
        slabs = range(c * step, (c + 1) * step)
        span = slice(c * step * LANES, (c + 1) * step * LANES)
        x = x + lax.dot_general(
            jnp.concatenate([held[k, :tokens, :] for k in slabs], axis=1),
            inp_ref[:, span],
            (((1,), (1,)), ((), ())),
            preferred_element_type=F32,
        )
        y = y + jnp.dot(
            jnp.concatenate([held[k, tokens:, :] for k in slabs], axis=1),
            outp_ref[span, :],
            preferred_element_type=F32,
        )
    drive[...] = x
    adj_in[...] = y
    for copy in others:
        copy.wait()
    dec_ref, near_ref, far_ref, w_ad, w_a, w_b = [kept.at[n] for n in range(6)]
    state = drive[strand(0, tokens), :]
    st_ref[strand(0, tokens), :] = state
    for j in range(1, steps):
        at = strand(j, tokens)
        state = dec_ref[at, :] * state + drive[at, :]
        st_ref[at, :] = state
    adjoint = adj_in[strand(steps - 1, tokens), :]
    ad_ref[strand(steps - 1, tokens), :] = adjoint
    for j in reversed(range(steps - 1)):
        at = strand(j, tokens)
        adjoint = dec_ref[strand(j + 1, tokens), :] * adjoint + adj_in[at, :]
        ad_ref[at, :] = adjoint
    first = dec_ref[strand(0, tokens), :] * adjoint
    rows, entering = [], jnp.zeros((1, LANES), F32)
    for k in range(ROWS):
        rows.append(entering)
        entering = ends_ref[k : k + 1, :] * entering + state[k : k + 1]
    into = jnp.concatenate(rows, axis=0)
    rows, leaving = [None] * ROWS, jnp.zeros((1, LANES), F32)
    for k in reversed(range(ROWS)):
        rows[k] = leaving
        leaving = ends_ref[k : k + 1, :] * leaving + first[k : k + 1]
    back = jnp.concatenate(rows, axis=0)
    sums = [jnp.zeros((ROWS, LANES), F32)] * 3
    previous = into
    for j in range(steps):
        at = strand(j, tokens)
        state = st_ref[at, :] + near_ref[at, :] * into
        adjoint = ad_ref[at, :] + far_ref[at, :] * back
        st_ref[at, :] = state
        ad_ref[at, :] = adjoint
        sums = [
            sums[0] + w_ad[at, :] * adjoint * previous,
            sums[1] + w_a[at, :] * adjoint,
            sums[2] + w_b[at, :] * previous,
        ]
        previous = state
    sums = [jnp.sum(s, axis=0, keepdims=True) for s in sums]
    block = jnp.concatenate(
        [
            ends_ref[ROWS : ROWS + 1, :],
            entering,
            leaving,
            *sums,
            ends_ref[ROWS + 1 : ROWS + 2, :],
            jnp.zeros((1, LANES), F32),
        ],
        axis=0,
    )
    for s in range(carry_ref.shape[0]):
        carry_ref[s] = block


def products_kernel(
    me_ref, carry_ref, g_ref, st_ref, ad_ref, d_ref,
    half_ref, to_ref, rates_ref, into, back, held, sems, kept, kept_sems, grads_ref, to_sems,
):
    others = fetch(d_ref, (CUM, REM), kept, kept_sems)
    copies, step = fetch_parts(g_ref, held, sems)
    devices = carry_ref.shape[0]
    blocks, both, _ = g_ref.shape
    tokens = both // 2
    entering = jnp.zeros((1, LANES), F32)
    for s in range(devices):
        into[s : s + 1, :] = entering
        entering = carry_ref[s, 0:1, :] * entering + carry_ref[s, 1:2, :]
    leaving = jnp.zeros((1, LANES), F32)
    total = jnp.zeros((1, LANES), F32)
    for s in reversed(range(devices)):
        back[s : s + 1, :] = leaving
        here = into[s : s + 1, :]
        total = total + (
            carry_ref[s, 3:4, :]
            + carry_ref[s, 4:5, :] * here
            + leaving * (carry_ref[s, 5:6, :] + carry_ref[s, 6:7, :] * here)
        )
        leaving = carry_ref[s, 0:1, :] * leaving + carry_ref[s, 2:3, :]
    rates_ref[...] = -total
    me = me_ref[0]
    for copy in others:
        copy.wait()
    adjoint = (ad_ref[...] + kept[1] * back[pl.ds(me, 1), :]).astype(BF16)
    state = (st_ref[...] + kept[0] * into[pl.ds(me, 1), :]).astype(BF16)
    half_ref[...] = adjoint
    half = LANES // 2
    sent = []
    for k in range(0, blocks, 2):
        if k % step == 0:
            copies[k // step].wait()
        x = jnp.concatenate([held[k, :tokens, :], held[k + 1, :tokens, :]], axis=1)
        y = jnp.concatenate([held[k, tokens:, :], held[k + 1, tokens:, :]], axis=1)
        gi = lax.dot_general(adjoint, x, (((0,), (0,)), ((), ())), preferred_element_type=F32)
        go = lax.dot_general(state, y, (((0,), (0,)), ((), ())), preferred_element_type=F32)
        for q in range(2):
            lanes = slice(q * LANES, (q + 1) * LANES)
            a = gi[:, lanes].astype(BF16)
            b = go[:, lanes].T.astype(BF16)
            for r in range(2):
                rows = slice(r * half, (r + 1) * half)
                grads_ref[2 * (k + q) + r, :half, :] = a[rows]
                grads_ref[2 * (k + q) + r, half:, :] = b[rows]
        if (k + 2) % step == 0:
            c = k // step
            chunk = pl.ds(2 * c * step, 2 * step)
            sent.append(
                pltpu.make_async_copy(grads_ref.at[chunk], to_ref.at[chunk], to_sems.at[c])
            )
            sent[-1].start()
    for copy in sent:
        copy.wait()


def sum_kernel(parts_ref, out_ref):
    total = parts_ref[0].astype(F32)
    for s in range(1, parts_ref.shape[0]):
        total = total + parts_ref[s].astype(F32)
    out_ref[...] = total.astype(BF16)


def sum_and_repeat_kernel(parts_ref, out_ref):
    total = parts_ref[0].astype(F32)
    for s in range(1, parts_ref.shape[0]):
        total = total + parts_ref[s].astype(F32)
    total = total.astype(BF16)
    for s in range(out_ref.shape[0]):
        out_ref[s] = total


def repeat_kernel(part_ref, out_ref):
    for s in range(out_ref.shape[0]):
        out_ref[s] = part_ref[...]


def finish_kernel(half_ref, col_ref, parts_ref, out_ref, gi_ref, go_ref, held, sems):
    copies, step = fetch_parts(half_ref, held, sems)
    half = LANES // 2
    for k in range(parts_ref.shape[0] // 2):
        for r in range(2):
            rows = slice(r * half, (r + 1) * half)
            gi_ref[rows, k * LANES : (k + 1) * LANES] = parts_ref[2 * k + r, :half, :].astype(F32)
            rows = slice(k * LANES + r * half, k * LANES + (r + 1) * half)
            go_ref[rows, :] = parts_ref[2 * k + r, half:, :].astype(F32)
    total = 0.0
    for c, copy in enumerate(copies):
        copy.wait()
        slabs = range(c * step, (c + 1) * step)
        a = jnp.concatenate([held[k] for k in slabs], axis=1)
        w = jnp.concatenate([col_ref[k] for k in slabs], axis=0)
        total = total + jnp.dot(a, w, preferred_element_type=F32)
    out_ref[...] = total.astype(BF16)


def on_device(inputs, out_grad, in_proj, out_proj, rates, time_step):
    tokens = inputs.shape[0]
    features = in_proj.shape[1]
    blocks = lax.axis_size("state")
    devices = lax.axis_size("seq")
    outer = devices // INNER
    along_y = [[x * INNER + y for y in range(INNER)] for x in range(outer)]
    along_x = [[x * INNER + y for x in range(outer)] for y in range(INNER)]
    sds = jax.ShapeDtypeStruct
    seen = sds((tokens, LANES), F32)
    me = lax.axis_index("seq").astype(jnp.int32).reshape(1)

    def exchange(x, groups):
        return lax.all_to_all(x, "seq", 0, 0, tiled=True, axis_index_groups=groups)

    def parted(shape):
        return [pltpu.VMEM(shape, BF16), pltpu.SemaphoreType.DMA((PARTS,))]

    def kept(number):
        return [pltpu.VMEM((number, tokens, LANES), F32), pltpu.SemaphoreType.DMA((number,))]

    together = call(
        join_kernel,
        sds((2 * tokens, LANES), BF16),
        in_specs=[HBM] * 2,
        out_specs=HBM,
        scratch=[pltpu.VMEM((2 * tokens, LANES), BF16), pltpu.SemaphoreType.DMA((4,))],
        limit=60 * 1024 * 1024,
    )(inputs, out_grad)
    gathered = lax.all_gather(together, "state", axis=0)
    columns = lax.all_to_all(
        jnp.moveaxis(in_proj.reshape(LANES, blocks, LANES), 1, 0), "state", 0, 0, tiled=True
    )
    decays, ends = call(
        decays_kernel,
        (sds((KINDS, tokens, LANES), F32), sds((2 * ROWS, LANES), F32)),
        in_specs=[VMEM] * 2 + [ANY],
    )(time_step[:, None], rates[None, :], columns)
    states, adjoints, carry = call(
        scans_kernel,
        (seen, seen, sds((devices, ROWS, LANES), F32)),
        in_specs=[SMEM] + [HBM] * 3 + [ANY, VMEM],
        scratch=[pltpu.VMEM((tokens, LANES), F32)] * 2
        + parted(gathered.shape)
        + kept(6)
        + [
            pltpu.VMEM(in_proj.shape, BF16),
            pltpu.VMEM(out_proj.shape, BF16),
            pltpu.SemaphoreType.DMA((2,)),
        ],
        cost=estimate(4 * tokens * features * LANES, 7 << 20),
        limit=SCANS,
    )(me, gathered, in_proj, out_proj, decays, ends)
    carry = exchange(carry, None)
    half, grads, grad_rates = call(
        products_kernel,
        (
            sds((tokens, LANES), BF16),
            sds((devices, features * 2 // devices, LANES), BF16),
            sds((1, LANES), F32),
        ),
        in_specs=[SMEM, VMEM, HBM, VMEM, VMEM, ANY],
        out_specs=[VMEM, HBM, VMEM],
        scratch=[pltpu.VMEM((devices, LANES), F32)] * 2
        + parted(gathered.shape)
        + kept(2)
        + parted((devices, features * 2 // devices, LANES)),
        cost=estimate(4 * tokens * features * LANES, 7 << 20),
        limit=PRODS,
    )(me, carry, gathered, states, adjoints, decays)
    half_all = lax.all_gather(half, "state", axis=0)
    rows = grads.shape[1]
    part = sds((INNER * rows, LANES), BF16)
    grads = exchange(grads.reshape(outer, INNER * rows, LANES), along_x)
    grads = call(sum_kernel, part)(grads)
    grads = exchange(grads.reshape(INNER, rows, LANES), along_y)
    grads = call(sum_and_repeat_kernel, sds((INNER, rows, LANES), BF16))(grads)
    grads = exchange(grads, along_y)
    grads = call(repeat_kernel, sds((outer, *part.shape), BF16))(grads.reshape(part.shape))
    grads = exchange(grads, along_x).reshape(devices, rows, LANES)
    grad_inputs, grad_in, grad_out = call(
        finish_kernel,
        (
            sds((tokens, LANES), BF16),
            sds((LANES, features), F32),
            sds((features, LANES), F32),
        ),
        in_specs=[HBM, VMEM, VMEM],
        scratch=parted(half_all.shape),
        limit=FINISH,
    )(half_all, columns, grads)
    return grad_inputs, grad_in, grad_out, grad_rates[0]


def solution(mesh):
    placed = (
        P("seq", "state"),
        P("seq", "state"),
        P("state", None),
        P(None, "state"),
        P("state"),
        P("seq"),
    )
    return jax.shard_map(
        on_device,
        mesh=mesh,
        in_specs=placed,
        out_specs=(P("seq", "state"), P("state", None), P(None, "state"), P("state")),
        check_vma=False,
    )
```

```python
import jax
import jax.numpy as jnp
from jax import lax
from jax.experimental import pallas as pl
from jax.experimental.pallas import tpu as pltpu
from jax.sharding import PartitionSpec as P

F32 = jnp.float32
BF16 = jnp.bfloat16
LANES = 128
ROWS = 8
INNER = 8
LIMIT = 32 * 1024 * 1024
VMEM = pl.BlockSpec(memory_space=pltpu.VMEM)
SMEM = pl.BlockSpec(memory_space=pltpu.SMEM)
HBM = pl.BlockSpec(memory_space=pltpu.HBM)
SCANS = 48 * 1024 * 1024
PRODS = 48 * 1024 * 1024
ANY = pl.BlockSpec(memory_space=pl.ANY)
DECAY, NEAR, FAR, NEXT, FIRST, KINDS = range(6)
CUM, REM = range(2)


def call(kernel, out_shape, scratch=(), cost=None, limit=LIMIT, **specs):
    return pl.pallas_call(
        kernel,
        out_shape=out_shape,
        **specs,
        scratch_shapes=list(scratch),
        compiler_params=pltpu.CompilerParams(vmem_limit_bytes=limit),
        cost_estimate=cost,
    )


def estimate(flops, nbytes):
    return pl.CostEstimate(flops=flops, bytes_accessed=nbytes, transcendentals=0)


def strand(step, tokens):
    return pl.ds(step, ROWS, tokens // ROWS)


def by_rows(values, last_first):
    rows, total = [None] * ROWS, jnp.ones_like(values[0:1])
    for k in reversed(range(ROWS)) if last_first else range(ROWS):
        rows[k] = total
        total = total * values[k : k + 1]
    return jnp.concatenate(rows, axis=0), total


def decays_kernel(
    dt_ref, next_ref, rates_ref, inp_ref, outp_ref, col_ref, d_ref, b_ref, ends_ref
):
    tokens = dt_ref.shape[0]
    steps = tokens // ROWS
    dec_ref, near_ref, far_ref = d_ref.at[DECAY], d_ref.at[NEAR], d_ref.at[FAR]
    cum_ref, rem_ref = b_ref.at[CUM], b_ref.at[REM]
    dec_ref[...] = jnp.exp(-dt_ref[...] * rates_ref[...])
    total = dec_ref[strand(0, tokens), :]
    near_ref[strand(0, tokens), :] = total
    for j in range(1, steps):
        total = total * dec_ref[strand(j, tokens), :]
        near_ref[strand(j, tokens), :] = total
    ahead = jnp.ones_like(total)
    for j in reversed(range(steps)):
        far_ref[strand(j, tokens), :] = ahead
        ahead = ahead * dec_ref[strand(j, tokens), :]
    before, whole = by_rows(total, False)
    after, _ = by_rows(total, True)
    for j in range(steps):
        at = strand(j, tokens)
        cum_ref[at, :] = near_ref[at, :] * before
        rem_ref[at, :] = far_ref[at, :] * after
    d_ref[NEXT] = jnp.broadcast_to(next_ref[...], dec_ref.shape)
    d_ref[FIRST] = dt_ref[...] * cum_ref[...]
    ends_ref[:ROWS, :] = total
    summed = jnp.sum(jnp.broadcast_to(dt_ref[...], dec_ref.shape), axis=0, keepdims=True)
    ends_ref[ROWS:, :] = jnp.concatenate(
        [whole, whole * summed, jnp.zeros((ROWS - 2, LANES), F32)], axis=0
    )


PARTS = 4


def join_kernel(a_ref, b_ref, out_ref, held, sems):
    rows = a_ref.shape[0]
    stays = [pl.ds(n * rows, rows) for n in range(2)]
    comes = [
        pltpu.make_async_copy(ref, held.at[at], sems.at[n])
        for n, (ref, at) in enumerate(zip((a_ref, b_ref), stays))
    ]
    goes = [
        pltpu.make_async_copy(held.at[at], out_ref.at[at], sems.at[2 + n])
        for n, at in enumerate(stays)
    ]
    for copy in comes:
        copy.start()
    for come, go in zip(comes, goes):
        come.wait()
        go.start()
    for copy in goes:
        copy.wait()


def fetch_parts(g_ref, held, sems):
    step = g_ref.shape[0] // PARTS
    copies = [
        pltpu.make_async_copy(
            g_ref.at[pl.ds(c * step, step)], held.at[pl.ds(c * step, step)], sems.at[c]
        )
        for c in range(PARTS)
    ]
    for copy in copies:
        copy.start()
    return copies, step


def scans_kernel(
    me_ref, g_ref, inp_ref, outp_ref, d_ref, b_ref, ends_ref,
    st_ref, ad_ref, carry_ref, drive, adj_in, held, sems,
):
    copies, step = fetch_parts(g_ref, held, sems)
    tokens = st_ref.shape[0]
    steps = tokens // ROWS
    x, y = 0.0, 0.0
    for c, copy in enumerate(copies):
        copy.wait()
        slabs = range(c * step, (c + 1) * step)
        span = slice(c * step * LANES, (c + 1) * step * LANES)
        x = x + lax.dot_general(
            jnp.concatenate([held[k, :tokens, :] for k in slabs], axis=1),
            inp_ref[:, span],
            (((1,), (1,)), ((), ())),
            preferred_element_type=F32,
        )
        y = y + jnp.dot(
            jnp.concatenate([held[k, tokens:, :] for k in slabs], axis=1),
            outp_ref[span, :],
            preferred_element_type=F32,
        )
    drive[...] = x
    adj_in[...] = y
    dec_ref = d_ref.at[DECAY]
    state = drive[strand(0, tokens), :]
    st_ref[strand(0, tokens), :] = state
    for j in range(1, steps):
        at = strand(j, tokens)
        state = dec_ref[at, :] * state + drive[at, :]
        st_ref[at, :] = state
    reaching = jnp.zeros((ROWS, LANES), F32)
    ad_ref[strand(steps - 1, tokens), :] = reaching
    adjoint = adj_in[strand(steps - 1, tokens), :]
    for j in reversed(range(steps - 1)):
        at = strand(j, tokens)
        reaching = dec_ref[strand(j + 1, tokens), :] * adjoint
        ad_ref[at, :] = reaching
        adjoint = reaching + adj_in[at, :]
    first = dec_ref[strand(0, tokens), :] * adjoint
    into, entering = [], jnp.zeros((1, LANES), F32)
    for k in range(ROWS):
        into.append(entering)
        entering = ends_ref[k : k + 1, :] * entering + state[k : k + 1]
    back, leaving = [None] * ROWS, jnp.zeros((1, LANES), F32)
    for k in reversed(range(ROWS)):
        back[k] = leaving
        leaving = ends_ref[k : k + 1, :] * leaving + first[k : k + 1]
    sums = [jnp.zeros((ROWS, LANES), F32)] * 3
    for k in range(ROWS):
        for j in range(k * steps, (k + 1) * steps, ROWS):
            at = slice(j, j + ROWS)
            state = st_ref[at, :] + d_ref[NEAR, at, :] * into[k]
            reaching = ad_ref[at, :] + d_ref[FAR, at, :] * back[k]
            adjoint = adj_in[at, :] + reaching
            st_ref[at, :] = state
            ad_ref[at, :] = adjoint
            timed = d_ref[NEXT, at, :] * state
            sums = [
                sums[0] + timed * reaching,
                sums[1] + d_ref[FIRST, at, :] * adjoint,
                sums[2] + timed * b_ref[REM, at, :],
            ]
    sums = [jnp.sum(s, axis=0, keepdims=True) for s in sums]
    block = jnp.concatenate(
        [
            ends_ref[ROWS : ROWS + 1, :],
            entering,
            leaving,
            *sums,
            ends_ref[ROWS + 1 : ROWS + 2, :],
            jnp.zeros((1, LANES), F32),
        ],
        axis=0,
    )
    for s in range(carry_ref.shape[0]):
        carry_ref[s] = block


def products_kernel(
    me_ref, carry_ref, g_ref, st_ref, ad_ref, b_ref,
    half_ref, grads_ref, rates_ref, into, back, held, sems,
):
    copies, step = fetch_parts(g_ref, held, sems)
    devices = carry_ref.shape[0]
    blocks, both, _ = g_ref.shape
    tokens = both // 2
    entering = jnp.zeros((1, LANES), F32)
    for s in range(devices):
        into[s : s + 1, :] = entering
        entering = carry_ref[s, 0:1, :] * entering + carry_ref[s, 1:2, :]
    leaving = jnp.zeros((1, LANES), F32)
    total = jnp.zeros((1, LANES), F32)
    for s in reversed(range(devices)):
        back[s : s + 1, :] = leaving
        here = into[s : s + 1, :]
        total = total + (
            carry_ref[s, 3:4, :]
            + carry_ref[s, 4:5, :] * here
            + leaving * (carry_ref[s, 5:6, :] + carry_ref[s, 6:7, :] * here)
        )
        leaving = carry_ref[s, 0:1, :] * leaving + carry_ref[s, 2:3, :]
    rates_ref[...] = -total
    me = me_ref[0]
    adjoint = (ad_ref[...] + b_ref[REM] * back[pl.ds(me, 1), :]).astype(BF16)
    state = (st_ref[...] + b_ref[CUM] * into[pl.ds(me, 1), :]).astype(BF16)
    half_ref[...] = adjoint
    half = LANES // 2
    for k in range(0, blocks, 2):
        if k % step == 0:
            copies[k // step].wait()
        x = jnp.concatenate([held[k, :tokens, :], held[k + 1, :tokens, :]], axis=1)
        y = jnp.concatenate([held[k, tokens:, :], held[k + 1, tokens:, :]], axis=1)
        gi = lax.dot_general(adjoint, x, (((0,), (0,)), ((), ())), preferred_element_type=F32)
        go = lax.dot_general(state, y, (((0,), (0,)), ((), ())), preferred_element_type=F32)
        for q in range(2):
            lanes = slice(q * LANES, (q + 1) * LANES)
            a = gi[:, lanes].astype(BF16)
            b = go[:, lanes].T.astype(BF16)
            for r in range(2):
                rows = slice(r * half, (r + 1) * half)
                grads_ref[2 * (k + q) + r, :half, :] = a[rows]
                grads_ref[2 * (k + q) + r, half:, :] = b[rows]


def sum_kernel(parts_ref, out_ref):
    total = parts_ref[0].astype(F32)
    for s in range(1, parts_ref.shape[0]):
        total = total + parts_ref[s].astype(F32)
    out_ref[...] = total.astype(BF16)


def sum_and_repeat_kernel(parts_ref, out_ref):
    total = parts_ref[0].astype(F32)
    for s in range(1, parts_ref.shape[0]):
        total = total + parts_ref[s].astype(F32)
    total = total.astype(BF16)
    for s in range(out_ref.shape[0]):
        out_ref[s] = total


def repeat_kernel(part_ref, out_ref):
    for s in range(out_ref.shape[0]):
        out_ref[s] = part_ref[...]


def inputs_kernel(half_ref, col_ref, out_ref, done_ref):
    done_ref[...] = jnp.zeros_like(done_ref)
    blocks = half_ref.shape[0]
    a = jnp.concatenate([half_ref[k] for k in range(blocks)], axis=1)
    w = jnp.concatenate([col_ref[k] for k in range(blocks)], axis=0)
    out_ref[...] = jnp.dot(a, w, preferred_element_type=F32).astype(BF16)


def finish_kernel(parts_ref, done_ref, gi_ref, go_ref):
    half = LANES // 2
    for k in range(parts_ref.shape[0] // 2):
        for r in range(2):
            rows = slice(r * half, (r + 1) * half)
            gi_ref[rows, k * LANES : (k + 1) * LANES] = parts_ref[2 * k + r, :half, :].astype(F32)
            rows = slice(k * LANES + r * half, k * LANES + (r + 1) * half)
            go_ref[rows, :] = parts_ref[2 * k + r, half:, :].astype(F32)


def on_device(inputs, out_grad, in_proj, out_proj, rates, time_step):
    tokens = inputs.shape[0]
    features = in_proj.shape[1]
    blocks = lax.axis_size("state")
    devices = lax.axis_size("seq")
    outer = devices // INNER
    along_y = [[x * INNER + y for y in range(INNER)] for x in range(outer)]
    along_x = [[x * INNER + y for x in range(outer)] for y in range(INNER)]
    sds = jax.ShapeDtypeStruct
    seen = sds((tokens, LANES), F32)
    me = lax.axis_index("seq").astype(jnp.int32).reshape(1)

    def exchange(x, groups):
        return lax.all_to_all(x, "seq", 0, 0, tiled=True, axis_index_groups=groups)

    def parted(shape):
        return [pltpu.VMEM(shape, BF16), pltpu.SemaphoreType.DMA((PARTS,))]

    together = call(
        join_kernel,
        sds((2 * tokens, LANES), BF16),
        in_specs=[HBM] * 2,
        out_specs=HBM,
        scratch=[pltpu.VMEM((2 * tokens, LANES), BF16), pltpu.SemaphoreType.DMA((4,))],
        limit=60 * 1024 * 1024,
    )(inputs, out_grad)
    gathered = lax.all_gather(together, "state", axis=0)
    columns = lax.all_to_all(
        jnp.moveaxis(in_proj.reshape(LANES, blocks, LANES), 1, 0), "state", 0, 0, tiled=True
    )
    following = jnp.concatenate([time_step[1:], jnp.zeros((1,), F32)])
    decays, whole, ends = call(
        decays_kernel,
        (
            sds((KINDS, tokens, LANES), F32),
            sds((2, tokens, LANES), F32),
            sds((2 * ROWS, LANES), F32),
        ),
        in_specs=[VMEM] * 5 + [ANY],
    )(time_step[:, None], following[:, None], rates[None, :], in_proj, out_proj, columns)
    states, adjoints, carry = call(
        scans_kernel,
        (seen, seen, sds((devices, ROWS, LANES), F32)),
        in_specs=[SMEM, HBM] + [VMEM] * 5,
        scratch=[pltpu.VMEM((tokens, LANES), F32)] * 2
        + parted(gathered.shape),
        cost=estimate(4 * tokens * features * LANES, 7 << 20),
        limit=SCANS,
    )(me, gathered, in_proj, out_proj, decays, whole, ends)
    carry = exchange(carry, None)
    half, grads, grad_rates = call(
        products_kernel,
        (
            sds((tokens, LANES), BF16),
            sds((devices, features * 2 // devices, LANES), BF16),
            sds((1, LANES), F32),
        ),
        in_specs=[SMEM, VMEM, HBM, VMEM, VMEM, VMEM],
        scratch=[pltpu.VMEM((devices, LANES), F32)] * 2 + parted(gathered.shape),
        cost=estimate(4 * tokens * features * LANES, 7 << 20),
        limit=PRODS,
    )(me, carry, gathered, states, adjoints, whole)
    half_all = lax.all_gather(half, "state", axis=0)
    rows = grads.shape[1]
    part = sds((INNER * rows, LANES), BF16)
    grads = exchange(grads.reshape(outer, INNER * rows, LANES), along_x)
    grads = call(sum_kernel, part)(grads)
    grads = exchange(grads.reshape(INNER, rows, LANES), along_y)
    grads = call(sum_and_repeat_kernel, sds((INNER, rows, LANES), BF16))(grads)
    grads = exchange(grads, along_y)
    grads = call(repeat_kernel, sds((outer, *part.shape), BF16))(grads.reshape(part.shape))
    grads = exchange(grads, along_x).reshape(devices, rows, LANES)
    grad_inputs, done = call(
        inputs_kernel,
        (sds((tokens, LANES), BF16), sds((ROWS, LANES), F32)),
        cost=estimate(2 * tokens * features * LANES, 3 << 20),
    )(half_all, columns)
    grad_in, grad_out = call(
        finish_kernel,
        (sds((LANES, features), F32), sds((features, LANES), F32)),
        in_specs=[VMEM, ANY],
    )(grads, done)
    return grad_inputs, grad_in, grad_out, grad_rates[0]


def solution(mesh):
    placed = (
        P("seq", "state"),
        P("seq", "state"),
        P("state", None),
        P(None, "state"),
        P("state"),
        P("seq"),
    )
    return jax.shard_map(
        on_device,
        mesh=mesh,
        in_specs=placed,
        out_specs=(P("seq", "state"), P("state", None), P(None, "state"), P("state")),
        check_vma=False,
    )
```

```python
import jax
import jax.numpy as jnp
from jax import lax
from jax.experimental import pallas as pl
from jax.experimental.pallas import tpu as pltpu
from jax.sharding import PartitionSpec as P

F32 = jnp.float32
BF16 = jnp.bfloat16
LANES = 128
ROWS = 8
INNER = 8
LIMIT = 32 * 1024 * 1024
VMEM = pl.BlockSpec(memory_space=pltpu.VMEM)
SMEM = pl.BlockSpec(memory_space=pltpu.SMEM)
HBM = pl.BlockSpec(memory_space=pltpu.HBM)
SCANS = 48 * 1024 * 1024
PRODS = 48 * 1024 * 1024
ANY = pl.BlockSpec(memory_space=pl.ANY)
DECAY, NEAR, FAR, NEXT, FIRST, KINDS = range(6)
CUM, REM = range(2)


def call(kernel, out_shape, scratch=(), cost=None, limit=LIMIT, **specs):
    return pl.pallas_call(
        kernel,
        out_shape=out_shape,
        **specs,
        scratch_shapes=list(scratch),
        compiler_params=pltpu.CompilerParams(vmem_limit_bytes=limit),
        cost_estimate=cost,
    )


def estimate(flops, nbytes):
    return pl.CostEstimate(flops=flops, bytes_accessed=nbytes, transcendentals=0)


def strand(step, tokens):
    return pl.ds(step, ROWS, tokens // ROWS)


def by_rows(values, last_first):
    rows, total = [None] * ROWS, jnp.ones_like(values[0:1])
    for k in reversed(range(ROWS)) if last_first else range(ROWS):
        rows[k] = total
        total = total * values[k : k + 1]
    return jnp.concatenate(rows, axis=0), total


def decays_kernel(
    dt_ref, next_ref, rates_ref, inp_ref, outp_ref, col_ref, d_ref, b_ref, ends_ref
):
    tokens = dt_ref.shape[0]
    steps = tokens // ROWS
    dec_ref, near_ref, far_ref = d_ref.at[DECAY], d_ref.at[NEAR], d_ref.at[FAR]
    cum_ref, rem_ref = b_ref.at[CUM], b_ref.at[REM]
    dec_ref[...] = jnp.exp(-dt_ref[...] * rates_ref[...])
    total = dec_ref[strand(0, tokens), :]
    near_ref[strand(0, tokens), :] = total
    for j in range(1, steps):
        total = total * dec_ref[strand(j, tokens), :]
        near_ref[strand(j, tokens), :] = total
    ahead = jnp.ones_like(total)
    for j in reversed(range(steps)):
        far_ref[strand(j, tokens), :] = ahead
        ahead = ahead * dec_ref[strand(j, tokens), :]
    before, whole = by_rows(total, False)
    after, _ = by_rows(total, True)
    for j in range(steps):
        at = strand(j, tokens)
        cum_ref[at, :] = near_ref[at, :] * before
        rem_ref[at, :] = far_ref[at, :] * after
    d_ref[NEXT] = jnp.broadcast_to(next_ref[...], dec_ref.shape)
    d_ref[FIRST] = dt_ref[...] * cum_ref[...]
    ends_ref[:ROWS, :] = total
    summed = jnp.sum(jnp.broadcast_to(dt_ref[...], dec_ref.shape), axis=0, keepdims=True)
    ends_ref[ROWS:, :] = jnp.concatenate(
        [whole, whole * summed, jnp.zeros((ROWS - 2, LANES), F32)], axis=0
    )


PARTS = 4


def join_kernel(a_ref, b_ref, out_ref, held, sems):
    rows = a_ref.shape[0]
    stays = [pl.ds(n * rows, rows) for n in range(2)]
    comes = [
        pltpu.make_async_copy(ref, held.at[at], sems.at[n])
        for n, (ref, at) in enumerate(zip((a_ref, b_ref), stays))
    ]
    goes = [
        pltpu.make_async_copy(held.at[at], out_ref.at[at], sems.at[2 + n])
        for n, at in enumerate(stays)
    ]
    for copy in comes:
        copy.start()
    for come, go in zip(comes, goes):
        come.wait()
        go.start()
    for copy in goes:
        copy.wait()


def fetch_parts(g_ref, held, sems):
    step = g_ref.shape[0] // PARTS
    copies = [
        pltpu.make_async_copy(
            g_ref.at[pl.ds(c * step, step)], held.at[pl.ds(c * step, step)], sems.at[c]
        )
        for c in range(PARTS)
    ]
    for copy in copies:
        copy.start()
    return copies, step


def scans_kernel(
    me_ref, g_ref, inp_ref, outp_ref, d_ref, b_ref, ends_ref,
    st_ref, ad_ref, carry_ref, drive, adj_in, held, sems,
):
    copies, step = fetch_parts(g_ref, held, sems)
    tokens = st_ref.shape[0]
    steps = tokens // ROWS
    x, y = 0.0, 0.0
    for c, copy in enumerate(copies):
        copy.wait()
        slabs = range(c * step, (c + 1) * step)
        span = slice(c * step * LANES, (c + 1) * step * LANES)
        x = x + lax.dot_general(
            jnp.concatenate([held[k, :tokens, :] for k in slabs], axis=1),
            inp_ref[:, span],
            (((1,), (1,)), ((), ())),
            preferred_element_type=F32,
        )
        y = y + jnp.dot(
            jnp.concatenate([held[k, tokens:, :] for k in slabs], axis=1),
            outp_ref[span, :],
            preferred_element_type=F32,
        )
    drive[...] = x
    adj_in[...] = y
    dec_ref = d_ref.at[DECAY]
    state = drive[strand(0, tokens), :]
    st_ref[strand(0, tokens), :] = state
    for j in range(1, steps):
        at = strand(j, tokens)
        state = dec_ref[at, :] * state + drive[at, :]
        st_ref[at, :] = state
    reaching = jnp.zeros((ROWS, LANES), F32)
    ad_ref[strand(steps - 1, tokens), :] = reaching
    adjoint = adj_in[strand(steps - 1, tokens), :]
    for j in reversed(range(steps - 1)):
        at = strand(j, tokens)
        reaching = dec_ref[strand(j + 1, tokens), :] * adjoint
        ad_ref[at, :] = reaching
        adjoint = reaching + adj_in[at, :]
    first = dec_ref[strand(0, tokens), :] * adjoint
    into, entering = [], jnp.zeros((1, LANES), F32)
    for k in range(ROWS):
        into.append(entering)
        entering = ends_ref[k : k + 1, :] * entering + state[k : k + 1]
    back, leaving = [None] * ROWS, jnp.zeros((1, LANES), F32)
    for k in reversed(range(ROWS)):
        back[k] = leaving
        leaving = ends_ref[k : k + 1, :] * leaving + first[k : k + 1]
    sums = [jnp.zeros((ROWS, LANES), F32)] * 3
    for k in range(ROWS):
        for j in range(k * steps, (k + 1) * steps, ROWS):
            at = slice(j, j + ROWS)
            state = st_ref[at, :] + d_ref[NEAR, at, :] * into[k]
            reaching = ad_ref[at, :] + d_ref[FAR, at, :] * back[k]
            adjoint = adj_in[at, :] + reaching
            st_ref[at, :] = state
            ad_ref[at, :] = adjoint
            timed = d_ref[NEXT, at, :] * state
            sums = [
                sums[0] + timed * reaching,
                sums[1] + d_ref[FIRST, at, :] * adjoint,
                sums[2] + timed * b_ref[REM, at, :],
            ]
    sums = [jnp.sum(s, axis=0, keepdims=True) for s in sums]
    block = jnp.concatenate(
        [
            ends_ref[ROWS : ROWS + 1, :],
            entering,
            leaving,
            *sums,
            ends_ref[ROWS + 1 : ROWS + 2, :],
            jnp.zeros((1, LANES), F32),
        ],
        axis=0,
    )
    for s in range(carry_ref.shape[0]):
        carry_ref[s] = block


def products_kernel(
    me_ref, carry_ref, g_ref, st_ref, ad_ref, b_ref,
    half_ref, grads_ref, rates_ref, into, back, held, sems,
):
    copies, step = fetch_parts(g_ref, held, sems)
    devices = carry_ref.shape[0]
    blocks, both, _ = g_ref.shape
    tokens = both // 2
    entering = jnp.zeros((1, LANES), F32)
    for s in range(devices):
        into[s : s + 1, :] = entering
        entering = carry_ref[s, 0:1, :] * entering + carry_ref[s, 1:2, :]
    leaving = jnp.zeros((1, LANES), F32)
    total = jnp.zeros((1, LANES), F32)
    for s in reversed(range(devices)):
        back[s : s + 1, :] = leaving
        here = into[s : s + 1, :]
        total = total + (
            carry_ref[s, 3:4, :]
            + carry_ref[s, 4:5, :] * here
            + leaving * (carry_ref[s, 5:6, :] + carry_ref[s, 6:7, :] * here)
        )
        leaving = carry_ref[s, 0:1, :] * leaving + carry_ref[s, 2:3, :]
    rates_ref[...] = -total
    me = me_ref[0]
    adjoint = (ad_ref[...] + b_ref[REM] * back[pl.ds(me, 1), :]).astype(BF16)
    state = (st_ref[...] + b_ref[CUM] * into[pl.ds(me, 1), :]).astype(BF16)
    half_ref[...] = adjoint
    half = LANES // 2
    for k in range(0, blocks, 2):
        if k % step == 0:
            copies[k // step].wait()
        x = jnp.concatenate([held[k, :tokens, :], held[k + 1, :tokens, :]], axis=1)
        y = jnp.concatenate([held[k, tokens:, :], held[k + 1, tokens:, :]], axis=1)
        gi = lax.dot_general(adjoint, x, (((0,), (0,)), ((), ())), preferred_element_type=F32)
        go = lax.dot_general(state, y, (((0,), (0,)), ((), ())), preferred_element_type=F32)
        for q in range(2):
            lanes = slice(q * LANES, (q + 1) * LANES)
            a = gi[:, lanes].astype(BF16)
            b = go[:, lanes].T.astype(BF16)
            for r in range(2):
                rows = slice(r * half, (r + 1) * half)
                grads_ref[2 * (k + q) + r, :half, :] = a[rows]
                grads_ref[2 * (k + q) + r, half:, :] = b[rows]


def sum_kernel(parts_ref, out_ref):
    total = parts_ref[0].astype(F32)
    for s in range(1, parts_ref.shape[0]):
        total = total + parts_ref[s].astype(F32)
    out_ref[...] = total.astype(BF16)


def sum_and_repeat_kernel(parts_ref, out_ref):
    total = parts_ref[0].astype(F32)
    for s in range(1, parts_ref.shape[0]):
        total = total + parts_ref[s].astype(F32)
    total = total.astype(BF16)
    for s in range(out_ref.shape[0]):
        out_ref[s] = total


def repeat_kernel(part_ref, out_ref):
    for s in range(out_ref.shape[0]):
        out_ref[s] = part_ref[...]


def inputs_kernel(half_ref, col_ref, out_ref, done_ref):
    done_ref[...] = jnp.zeros_like(done_ref)
    blocks = half_ref.shape[0]
    a = jnp.concatenate([half_ref[k] for k in range(blocks)], axis=1)
    w = jnp.concatenate(
        [col_ref[y, k] for k in range(blocks) for y in range(col_ref.shape[0])], axis=0
    )
    out_ref[...] = jnp.dot(a, w, preferred_element_type=F32).astype(BF16)


def finish_kernel(parts_ref, done_ref, gi_ref, go_ref):
    half = LANES // 2
    for k in range(parts_ref.shape[0] // 2):
        for r in range(2):
            rows = slice(r * half, (r + 1) * half)
            gi_ref[rows, k * LANES : (k + 1) * LANES] = parts_ref[2 * k + r, :half, :].astype(F32)
            rows = slice(k * LANES + r * half, k * LANES + (r + 1) * half)
            go_ref[rows, :] = parts_ref[2 * k + r, half:, :].astype(F32)


def on_device(inputs, out_grad, in_proj, out_proj, rates, time_step):
    tokens = inputs.shape[0]
    features = in_proj.shape[1]
    blocks = lax.axis_size("state")
    devices = lax.axis_size("seq")
    outer = devices // INNER
    along_y = [[x * INNER + y for y in range(INNER)] for x in range(outer)]
    along_x = [[x * INNER + y for x in range(outer)] for y in range(INNER)]
    sds = jax.ShapeDtypeStruct
    seen = sds((tokens, LANES), F32)
    me = lax.axis_index("seq").astype(jnp.int32).reshape(1)

    def exchange(x, groups):
        return lax.all_to_all(x, "seq", 0, 0, tiled=True, axis_index_groups=groups)

    def parted(shape):
        return [pltpu.VMEM(shape, BF16), pltpu.SemaphoreType.DMA((PARTS,))]

    together = call(
        join_kernel,
        sds((2 * tokens, LANES), BF16),
        in_specs=[HBM] * 2,
        out_specs=HBM,
        scratch=[pltpu.VMEM((2 * tokens, LANES), BF16), pltpu.SemaphoreType.DMA((4,))],
        limit=60 * 1024 * 1024,
    )(inputs, out_grad)
    gathered = lax.all_gather(together, "state", axis=0)
    rows = LANES // INNER
    place = lax.rem(lax.axis_index("seq").astype(jnp.int32), jnp.int32(INNER))
    columns = lax.dynamic_slice_in_dim(in_proj, place * rows, rows, 0)
    columns = jnp.moveaxis(columns.reshape(rows, blocks, LANES), 1, 0)
    columns = lax.all_to_all(columns, "state", 0, 0, tiled=True)
    columns = exchange(jnp.broadcast_to(columns, (INNER, *columns.shape)), along_y)
    following = jnp.concatenate([time_step[1:], jnp.zeros((1,), F32)])
    decays, whole, ends = call(
        decays_kernel,
        (
            sds((KINDS, tokens, LANES), F32),
            sds((2, tokens, LANES), F32),
            sds((2 * ROWS, LANES), F32),
        ),
        in_specs=[VMEM] * 5 + [ANY],
    )(time_step[:, None], following[:, None], rates[None, :], in_proj, out_proj, columns)
    states, adjoints, carry = call(
        scans_kernel,
        (seen, seen, sds((devices, ROWS, LANES), F32)),
        in_specs=[SMEM, HBM] + [VMEM] * 5,
        scratch=[pltpu.VMEM((tokens, LANES), F32)] * 2
        + parted(gathered.shape),
        cost=estimate(4 * tokens * features * LANES, 7 << 20),
        limit=SCANS,
    )(me, gathered, in_proj, out_proj, decays, whole, ends)
    carry = exchange(carry, None)
    half, grads, grad_rates = call(
        products_kernel,
        (
            sds((tokens, LANES), BF16),
            sds((devices, features * 2 // devices, LANES), BF16),
            sds((1, LANES), F32),
        ),
        in_specs=[SMEM, VMEM, HBM, VMEM, VMEM, VMEM],
        scratch=[pltpu.VMEM((devices, LANES), F32)] * 2 + parted(gathered.shape),
        cost=estimate(4 * tokens * features * LANES, 7 << 20),
        limit=PRODS,
    )(me, carry, gathered, states, adjoints, whole)
    half_all = lax.all_gather(half, "state", axis=0)
    rows = grads.shape[1]
    part = sds((INNER * rows, LANES), BF16)
    grads = exchange(grads.reshape(outer, INNER * rows, LANES), along_x)
    grads = call(sum_kernel, part)(grads)
    grads = exchange(grads.reshape(INNER, rows, LANES), along_y)
    grads = call(sum_and_repeat_kernel, sds((INNER, rows, LANES), BF16))(grads)
    grads = exchange(grads, along_y)
    grads = call(repeat_kernel, sds((outer, *part.shape), BF16))(grads.reshape(part.shape))
    grads = exchange(grads, along_x).reshape(devices, rows, LANES)
    grad_inputs, done = call(
        inputs_kernel,
        (sds((tokens, LANES), BF16), sds((ROWS, LANES), F32)),
        cost=estimate(2 * tokens * features * LANES, 3 << 20),
    )(half_all, columns)
    grad_in, grad_out = call(
        finish_kernel,
        (sds((LANES, features), F32), sds((features, LANES), F32)),
        in_specs=[VMEM, ANY],
    )(grads, done)
    return grad_inputs, grad_in, grad_out, grad_rates[0]


def solution(mesh):
    placed = (
        P("seq", "state"),
        P("seq", "state"),
        P("state", None),
        P(None, "state"),
        P("state"),
        P("seq"),
    )
    return jax.shard_map(
        on_device,
        mesh=mesh,
        in_specs=placed,
        out_specs=(P("seq", "state"), P("state", None), P(None, "state"), P("state")),
        check_vma=False,
    )
```

```python
import jax
import jax.numpy as jnp
from jax import lax
from jax.experimental import pallas as pl
from jax.experimental.pallas import tpu as pltpu
from jax.sharding import PartitionSpec as P

F32 = jnp.float32
BF16 = jnp.bfloat16
LANES = 128
ROWS = 8
INNER = 8
LIMIT = 32 * 1024 * 1024
VMEM = pl.BlockSpec(memory_space=pltpu.VMEM)
SMEM = pl.BlockSpec(memory_space=pltpu.SMEM)
HBM = pl.BlockSpec(memory_space=pltpu.HBM)
SCANS = 46 * 1024 * 1024
PRODS = 46 * 1024 * 1024
ANY = pl.BlockSpec(memory_space=pl.ANY)
DECAY, NEAR, FAR, NEXT, FIRST, KINDS = range(6)
CUM, REM = range(2)


def call(kernel, out_shape, scratch=(), cost=None, limit=LIMIT, **specs):
    return pl.pallas_call(
        kernel,
        out_shape=out_shape,
        **specs,
        scratch_shapes=list(scratch),
        compiler_params=pltpu.CompilerParams(vmem_limit_bytes=limit),
        cost_estimate=cost,
    )


def estimate(flops, nbytes):
    return pl.CostEstimate(flops=flops, bytes_accessed=nbytes, transcendentals=0)


def strand(step, tokens):
    return pl.ds(step, ROWS, tokens // ROWS)


def by_rows(values, last_first):
    rows, total = [None] * ROWS, jnp.ones_like(values[0:1])
    for k in reversed(range(ROWS)) if last_first else range(ROWS):
        rows[k] = total
        total = total * values[k : k + 1]
    return jnp.concatenate(rows, axis=0), total


def decays_kernel(
    dt_ref, next_ref, rates_ref, inp_ref, outp_ref, col_ref, d_ref, b_ref, ends_ref
):
    tokens = dt_ref.shape[0]
    steps = tokens // ROWS
    dec_ref, near_ref, far_ref = d_ref.at[DECAY], d_ref.at[NEAR], d_ref.at[FAR]
    cum_ref, rem_ref = b_ref.at[CUM], b_ref.at[REM]
    dec_ref[...] = jnp.exp(-dt_ref[...] * rates_ref[...])
    total = dec_ref[strand(0, tokens), :]
    near_ref[strand(0, tokens), :] = total
    for j in range(1, steps):
        total = total * dec_ref[strand(j, tokens), :]
        near_ref[strand(j, tokens), :] = total
    ahead = jnp.ones_like(total)
    for j in reversed(range(steps)):
        far_ref[strand(j, tokens), :] = ahead
        ahead = ahead * dec_ref[strand(j, tokens), :]
    before, whole = by_rows(total, False)
    after, _ = by_rows(total, True)
    for j in range(steps):
        at = strand(j, tokens)
        cum_ref[at, :] = near_ref[at, :] * before
        rem_ref[at, :] = far_ref[at, :] * after
    d_ref[NEXT] = jnp.broadcast_to(next_ref[...], dec_ref.shape)
    d_ref[FIRST] = dt_ref[...] * cum_ref[...]
    ends_ref[:ROWS, :] = total
    summed = jnp.sum(jnp.broadcast_to(dt_ref[...], dec_ref.shape), axis=0, keepdims=True)
    ends_ref[ROWS:, :] = jnp.concatenate(
        [whole, whole * summed, jnp.zeros((ROWS - 2, LANES), F32)], axis=0
    )


PARTS = 4


def join_kernel(a_ref, b_ref, out_ref, held, sems):
    rows = a_ref.shape[0]
    stays = [pl.ds(n * rows, rows) for n in range(2)]
    comes = [
        pltpu.make_async_copy(ref, held.at[at], sems.at[n])
        for n, (ref, at) in enumerate(zip((a_ref, b_ref), stays))
    ]
    goes = [
        pltpu.make_async_copy(held.at[at], out_ref.at[at], sems.at[2 + n])
        for n, at in enumerate(stays)
    ]
    for copy in comes:
        copy.start()
    for come, go in zip(comes, goes):
        come.wait()
        go.start()
    for copy in goes:
        copy.wait()


def fetch_parts(g_ref, held, sems):
    step = g_ref.shape[0] // PARTS
    copies = [
        pltpu.make_async_copy(
            g_ref.at[pl.ds(c * step, step)], held.at[pl.ds(c * step, step)], sems.at[c]
        )
        for c in range(PARTS)
    ]
    for copy in copies:
        copy.start()
    return copies, step


def scans_kernel(
    me_ref, g_ref, inp_ref, outp_ref, d_ref, b_ref, ends_ref,
    st_ref, ad_ref, carry_ref, held, drive, adj_in, sems,
):
    copies, step = fetch_parts(g_ref, held, sems)
    tokens = st_ref.shape[0]
    steps = tokens // ROWS
    x, y = 0.0, 0.0
    for c, copy in enumerate(copies):
        copy.wait()
        slabs = range(c * step, (c + 1) * step)
        span = slice(c * step * LANES, (c + 1) * step * LANES)
        x = x + lax.dot_general(
            jnp.concatenate([held[k, :tokens, :] for k in slabs], axis=1),
            inp_ref[:, span],
            (((1,), (1,)), ((), ())),
            preferred_element_type=F32,
        )
        y = y + jnp.dot(
            jnp.concatenate([held[k, tokens:, :] for k in slabs], axis=1),
            outp_ref[span, :],
            preferred_element_type=F32,
        )
    drive[...] = x
    adj_in[...] = y
    dec_ref = d_ref.at[DECAY]
    state = drive[strand(0, tokens), :]
    st_ref[strand(0, tokens), :] = state
    for j in range(1, steps):
        at = strand(j, tokens)
        state = dec_ref[at, :] * state + drive[at, :]
        st_ref[at, :] = state
    reaching = jnp.zeros((ROWS, LANES), F32)
    ad_ref[strand(steps - 1, tokens), :] = reaching
    adjoint = adj_in[strand(steps - 1, tokens), :]
    for j in reversed(range(steps - 1)):
        at = strand(j, tokens)
        reaching = dec_ref[strand(j + 1, tokens), :] * adjoint
        ad_ref[at, :] = reaching
        adjoint = reaching + adj_in[at, :]
    first = dec_ref[strand(0, tokens), :] * adjoint
    into, entering = [], jnp.zeros((1, LANES), F32)
    for k in range(ROWS):
        into.append(entering)
        entering = ends_ref[k : k + 1, :] * entering + state[k : k + 1]
    back, leaving = [None] * ROWS, jnp.zeros((1, LANES), F32)
    for k in reversed(range(ROWS)):
        back[k] = leaving
        leaving = ends_ref[k : k + 1, :] * leaving + first[k : k + 1]
    sums = [jnp.zeros((ROWS, LANES), F32)] * 3
    for k in range(ROWS):
        for j in range(k * steps, (k + 1) * steps, ROWS):
            at = slice(j, j + ROWS)
            state = st_ref[at, :] + d_ref[NEAR, at, :] * into[k]
            reaching = ad_ref[at, :] + d_ref[FAR, at, :] * back[k]
            adjoint = adj_in[at, :] + reaching
            st_ref[at, :] = state
            ad_ref[at, :] = adjoint
            timed = d_ref[NEXT, at, :] * state
            sums = [
                sums[0] + timed * reaching,
                sums[1] + d_ref[FIRST, at, :] * adjoint,
                sums[2] + timed * b_ref[REM, at, :],
            ]
    sums = [jnp.sum(s, axis=0, keepdims=True) for s in sums]
    block = jnp.concatenate(
        [
            ends_ref[ROWS : ROWS + 1, :],
            entering,
            leaving,
            *sums,
            ends_ref[ROWS + 1 : ROWS + 2, :],
            jnp.zeros((1, LANES), F32),
        ],
        axis=0,
    )
    for s in range(carry_ref.shape[0]):
        carry_ref[s] = block


def products_kernel(
    me_ref, carry_ref, g_ref, st_ref, ad_ref, b_ref,
    half_ref, grads_ref, rates_ref, into, back,
):
    devices = carry_ref.shape[0]
    blocks, both, _ = g_ref.shape
    tokens = both // 2
    entering = jnp.zeros((1, LANES), F32)
    for s in range(devices):
        into[s : s + 1, :] = entering
        entering = carry_ref[s, 0:1, :] * entering + carry_ref[s, 1:2, :]
    leaving = jnp.zeros((1, LANES), F32)
    total = jnp.zeros((1, LANES), F32)
    for s in reversed(range(devices)):
        back[s : s + 1, :] = leaving
        here = into[s : s + 1, :]
        total = total + (
            carry_ref[s, 3:4, :]
            + carry_ref[s, 4:5, :] * here
            + leaving * (carry_ref[s, 5:6, :] + carry_ref[s, 6:7, :] * here)
        )
        leaving = carry_ref[s, 0:1, :] * leaving + carry_ref[s, 2:3, :]
    rates_ref[...] = -total
    me = me_ref[0]
    adjoint = (ad_ref[...] + b_ref[REM] * back[pl.ds(me, 1), :]).astype(BF16)
    state = (st_ref[...] + b_ref[CUM] * into[pl.ds(me, 1), :]).astype(BF16)
    half_ref[...] = adjoint
    half = LANES // 2
    for k in range(0, blocks, 2):
        x = jnp.concatenate([g_ref[k, :tokens, :], g_ref[k + 1, :tokens, :]], axis=1)
        y = jnp.concatenate([g_ref[k, tokens:, :], g_ref[k + 1, tokens:, :]], axis=1)
        gi = lax.dot_general(adjoint, x, (((0,), (0,)), ((), ())), preferred_element_type=F32)
        go = lax.dot_general(state, y, (((0,), (0,)), ((), ())), preferred_element_type=F32)
        for q in range(2):
            lanes = slice(q * LANES, (q + 1) * LANES)
            a = gi[:, lanes].astype(BF16)
            b = go[:, lanes].T.astype(BF16)
            for r in range(2):
                rows = slice(r * half, (r + 1) * half)
                grads_ref[2 * (k + q) + r, :half, :] = a[rows]
                grads_ref[2 * (k + q) + r, half:, :] = b[rows]


def sum_kernel(parts_ref, out_ref):
    total = parts_ref[0].astype(F32)
    for s in range(1, parts_ref.shape[0]):
        total = total + parts_ref[s].astype(F32)
    out_ref[...] = total.astype(BF16)


def sum_and_repeat_kernel(parts_ref, out_ref):
    total = parts_ref[0].astype(F32)
    for s in range(1, parts_ref.shape[0]):
        total = total + parts_ref[s].astype(F32)
    total = total.astype(BF16)
    for s in range(out_ref.shape[0]):
        out_ref[s] = total


def repeat_kernel(part_ref, out_ref):
    for s in range(out_ref.shape[0]):
        out_ref[s] = part_ref[...]


def inputs_kernel(half_ref, col_ref, out_ref, done_ref):
    done_ref[...] = jnp.zeros_like(done_ref)
    blocks = half_ref.shape[0]
    a = jnp.concatenate([half_ref[k] for k in range(blocks)], axis=1)
    w = jnp.concatenate(
        [col_ref[y, k] for k in range(blocks) for y in range(col_ref.shape[0])], axis=0
    )
    out_ref[...] = jnp.dot(a, w, preferred_element_type=F32).astype(BF16)


def finish_kernel(parts_ref, done_ref, gi_ref, go_ref):
    half = LANES // 2
    for k in range(parts_ref.shape[0] // 2):
        for r in range(2):
            rows = slice(r * half, (r + 1) * half)
            gi_ref[rows, k * LANES : (k + 1) * LANES] = parts_ref[2 * k + r, :half, :].astype(F32)
            rows = slice(k * LANES + r * half, k * LANES + (r + 1) * half)
            go_ref[rows, :] = parts_ref[2 * k + r, half:, :].astype(F32)


def on_device(inputs, out_grad, in_proj, out_proj, rates, time_step):
    tokens = inputs.shape[0]
    features = in_proj.shape[1]
    blocks = lax.axis_size("state")
    devices = lax.axis_size("seq")
    outer = devices // INNER
    along_y = [[x * INNER + y for y in range(INNER)] for x in range(outer)]
    along_x = [[x * INNER + y for x in range(outer)] for y in range(INNER)]
    sds = jax.ShapeDtypeStruct
    seen = sds((tokens, LANES), F32)
    me = lax.axis_index("seq").astype(jnp.int32).reshape(1)

    def exchange(x, groups):
        return lax.all_to_all(x, "seq", 0, 0, tiled=True, axis_index_groups=groups)

    def parted(shape):
        return [pltpu.VMEM(shape, BF16), pltpu.SemaphoreType.DMA((PARTS,))]

    together = call(
        join_kernel,
        sds((2 * tokens, LANES), BF16),
        in_specs=[HBM] * 2,
        out_specs=HBM,
        scratch=[pltpu.VMEM((2 * tokens, LANES), BF16), pltpu.SemaphoreType.DMA((4,))],
        limit=60 * 1024 * 1024,
    )(inputs, out_grad)
    gathered = lax.all_gather(together, "state", axis=0)
    rows = LANES // INNER
    place = lax.rem(lax.axis_index("seq").astype(jnp.int32), jnp.int32(INNER))
    columns = lax.dynamic_slice_in_dim(in_proj, place * rows, rows, 0)
    columns = jnp.moveaxis(columns.reshape(rows, blocks, LANES), 1, 0)
    columns = lax.all_to_all(columns, "state", 0, 0, tiled=True)
    columns = exchange(jnp.broadcast_to(columns, (INNER, *columns.shape)), along_y)
    following = jnp.concatenate([time_step[1:], jnp.zeros((1,), F32)])
    decays, whole, ends = call(
        decays_kernel,
        (
            sds((KINDS, tokens, LANES), F32),
            sds((2, tokens, LANES), F32),
            sds((2 * ROWS, LANES), F32),
        ),
        in_specs=[VMEM] * 5 + [ANY],
    )(time_step[:, None], following[:, None], rates[None, :], in_proj, out_proj, columns)
    states, adjoints, carry, gathered = call(
        scans_kernel,
        (seen, seen, sds((devices, ROWS, LANES), F32), sds(gathered.shape, BF16)),
        in_specs=[SMEM, HBM] + [VMEM] * 5,
        scratch=[pltpu.VMEM((tokens, LANES), F32)] * 2 + [pltpu.SemaphoreType.DMA((PARTS,))],
        cost=estimate(4 * tokens * features * LANES, 7 << 20),
        limit=SCANS,
    )(me, gathered, in_proj, out_proj, decays, whole, ends)
    carry = exchange(carry, None)
    half, grads, grad_rates = call(
        products_kernel,
        (
            sds((tokens, LANES), BF16),
            sds((devices, features * 2 // devices, LANES), BF16),
            sds((1, LANES), F32),
        ),
        in_specs=[SMEM] + [VMEM] * 5,
        scratch=[pltpu.VMEM((devices, LANES), F32)] * 2,
        cost=estimate(4 * tokens * features * LANES, 7 << 20),
        limit=PRODS,
    )(me, carry, gathered, states, adjoints, whole)
    half_all = lax.all_gather(half, "state", axis=0)
    rows = grads.shape[1]
    part = sds((INNER * rows, LANES), BF16)
    grads = exchange(grads.reshape(outer, INNER * rows, LANES), along_x)
    grads = call(sum_kernel, part)(grads)
    grads = exchange(grads.reshape(INNER, rows, LANES), along_y)
    grads = call(sum_and_repeat_kernel, sds((INNER, rows, LANES), BF16))(grads)
    grads = exchange(grads, along_y)
    grads = call(repeat_kernel, sds((outer, *part.shape), BF16))(grads.reshape(part.shape))
    grads = exchange(grads, along_x).reshape(devices, rows, LANES)
    grad_inputs, done = call(
        inputs_kernel,
        (sds((tokens, LANES), BF16), sds((ROWS, LANES), F32)),
        cost=estimate(2 * tokens * features * LANES, 3 << 20),
    )(half_all, columns)
    grad_in, grad_out = call(
        finish_kernel,
        (sds((LANES, features), F32), sds((features, LANES), F32)),
        in_specs=[VMEM, ANY],
    )(grads, done)
    return grad_inputs, grad_in, grad_out, grad_rates[0]


def solution(mesh):
    placed = (
        P("seq", "state"),
        P("seq", "state"),
        P("state", None),
        P(None, "state"),
        P("state"),
        P("seq"),
    )
    return jax.shard_map(
        on_device,
        mesh=mesh,
        in_specs=placed,
        out_specs=(P("seq", "state"), P("state", None), P(None, "state"), P("state")),
        check_vma=False,
    )
```

```python
import jax
import jax.numpy as jnp
from jax import lax
from jax.experimental import pallas as pl
from jax.experimental.pallas import tpu as pltpu
from jax.sharding import PartitionSpec as P

F32 = jnp.float32
BF16 = jnp.bfloat16
LANES = 128
ROWS = 8
INNER = 8
LIMIT = 32 * 1024 * 1024
VMEM = pl.BlockSpec(memory_space=pltpu.VMEM)
SMEM = pl.BlockSpec(memory_space=pltpu.SMEM)
HBM = pl.BlockSpec(memory_space=pltpu.HBM)
SCANS = 46 * 1024 * 1024
PRODS = 46 * 1024 * 1024
ANY = pl.BlockSpec(memory_space=pl.ANY)
DECAY, NEAR, FAR, NEXT, FIRST, KINDS = range(6)
CUM, REM = range(2)


def call(kernel, out_shape, scratch=(), cost=None, limit=LIMIT, **specs):
    return pl.pallas_call(
        kernel,
        out_shape=out_shape,
        **specs,
        scratch_shapes=list(scratch),
        compiler_params=pltpu.CompilerParams(vmem_limit_bytes=limit),
        cost_estimate=cost,
    )


def estimate(flops, nbytes):
    return pl.CostEstimate(flops=flops, bytes_accessed=nbytes, transcendentals=0)


def strand(step, tokens):
    return pl.ds(step, ROWS, tokens // ROWS)


def by_rows(values, last_first):
    rows, total = [None] * ROWS, jnp.ones_like(values[0:1])
    for k in reversed(range(ROWS)) if last_first else range(ROWS):
        rows[k] = total
        total = total * values[k : k + 1]
    return jnp.concatenate(rows, axis=0), total


def decays_kernel(
    dt_ref, next_ref, rates_ref, inp_ref, outp_ref, col_ref, d_ref, b_ref, ends_ref
):
    tokens = dt_ref.shape[0]
    steps = tokens // ROWS
    dec_ref, near_ref, far_ref = d_ref.at[DECAY], d_ref.at[NEAR], d_ref.at[FAR]
    cum_ref, rem_ref = b_ref.at[CUM], b_ref.at[REM]
    dec_ref[...] = jnp.exp(-dt_ref[...] * rates_ref[...])
    total = dec_ref[strand(0, tokens), :]
    near_ref[strand(0, tokens), :] = total
    for j in range(1, steps):
        total = total * dec_ref[strand(j, tokens), :]
        near_ref[strand(j, tokens), :] = total
    ahead = jnp.ones_like(total)
    for j in reversed(range(steps)):
        far_ref[strand(j, tokens), :] = ahead
        ahead = ahead * dec_ref[strand(j, tokens), :]
    before, whole = by_rows(total, False)
    after, _ = by_rows(total, True)
    for j in range(steps):
        at = strand(j, tokens)
        cum_ref[at, :] = near_ref[at, :] * before
        rem_ref[at, :] = far_ref[at, :] * after
    d_ref[NEXT] = jnp.broadcast_to(next_ref[...], dec_ref.shape)
    d_ref[FIRST] = dt_ref[...] * cum_ref[...]
    ends_ref[:ROWS, :] = total
    summed = jnp.sum(jnp.broadcast_to(dt_ref[...], dec_ref.shape), axis=0, keepdims=True)
    ends_ref[ROWS:, :] = jnp.concatenate(
        [whole, whole * summed, jnp.zeros((ROWS - 2, LANES), F32)], axis=0
    )


PARTS = 8


def join_kernel(a_ref, b_ref, out_ref, held, sems):
    rows = a_ref.shape[0]
    stays = [pl.ds(n * rows, rows) for n in range(2)]
    comes = [
        pltpu.make_async_copy(ref, held.at[at], sems.at[n])
        for n, (ref, at) in enumerate(zip((a_ref, b_ref), stays))
    ]
    goes = [
        pltpu.make_async_copy(held.at[at], out_ref.at[at], sems.at[2 + n])
        for n, at in enumerate(stays)
    ]
    for copy in comes:
        copy.start()
    for come, go in zip(comes, goes):
        come.wait()
        go.start()
    for copy in goes:
        copy.wait()


def fetch_parts(g_ref, held, sems):
    step = g_ref.shape[0] // PARTS
    copies = [
        pltpu.make_async_copy(
            g_ref.at[pl.ds(c * step, step)], held.at[pl.ds(c * step, step)], sems.at[c]
        )
        for c in range(PARTS)
    ]
    for copy in copies:
        copy.start()
    return copies, step


def scans_kernel(
    me_ref, g_ref, inp_ref, outp_ref, d_ref, b_ref, ends_ref,
    st_ref, ad_ref, carry_ref, held, drive, adj_in, sems,
):
    copies, step = fetch_parts(g_ref, held, sems)
    tokens = st_ref.shape[0]
    steps = tokens // ROWS
    x, y = 0.0, 0.0
    for c, copy in enumerate(copies):
        copy.wait()
        slabs = range(c * step, (c + 1) * step)
        span = slice(c * step * LANES, (c + 1) * step * LANES)
        x = x + lax.dot_general(
            jnp.concatenate([held[k, :tokens, :] for k in slabs], axis=1),
            inp_ref[:, span],
            (((1,), (1,)), ((), ())),
            preferred_element_type=F32,
        )
        y = y + jnp.dot(
            jnp.concatenate([held[k, tokens:, :] for k in slabs], axis=1),
            outp_ref[span, :],
            preferred_element_type=F32,
        )
    drive[...] = x
    adj_in[...] = y
    dec_ref = d_ref.at[DECAY]
    state = drive[strand(0, tokens), :]
    st_ref[strand(0, tokens), :] = state
    for j in range(1, steps):
        at = strand(j, tokens)
        state = dec_ref[at, :] * state + drive[at, :]
        st_ref[at, :] = state
    reaching = jnp.zeros((ROWS, LANES), F32)
    ad_ref[strand(steps - 1, tokens), :] = reaching
    adjoint = adj_in[strand(steps - 1, tokens), :]
    for j in reversed(range(steps - 1)):
        at = strand(j, tokens)
        reaching = dec_ref[strand(j + 1, tokens), :] * adjoint
        ad_ref[at, :] = reaching
        adjoint = reaching + adj_in[at, :]
    first = dec_ref[strand(0, tokens), :] * adjoint
    into, entering = [], jnp.zeros((1, LANES), F32)
    for k in range(ROWS):
        into.append(entering)
        entering = ends_ref[k : k + 1, :] * entering + state[k : k + 1]
    back, leaving = [None] * ROWS, jnp.zeros((1, LANES), F32)
    for k in reversed(range(ROWS)):
        back[k] = leaving
        leaving = ends_ref[k : k + 1, :] * leaving + first[k : k + 1]
    sums = [jnp.zeros((ROWS, LANES), F32)] * 3
    for k in range(ROWS):
        for j in range(k * steps, (k + 1) * steps, ROWS):
            at = slice(j, j + ROWS)
            state = st_ref[at, :] + d_ref[NEAR, at, :] * into[k]
            reaching = ad_ref[at, :] + d_ref[FAR, at, :] * back[k]
            adjoint = adj_in[at, :] + reaching
            st_ref[at, :] = state
            ad_ref[at, :] = adjoint
            timed = d_ref[NEXT, at, :] * state
            sums = [
                sums[0] + timed * reaching,
                sums[1] + d_ref[FIRST, at, :] * adjoint,
                sums[2] + timed * b_ref[REM, at, :],
            ]
    sums = [jnp.sum(s, axis=0, keepdims=True) for s in sums]
    block = jnp.concatenate(
        [
            ends_ref[ROWS : ROWS + 1, :],
            entering,
            leaving,
            *sums,
            ends_ref[ROWS + 1 : ROWS + 2, :],
            jnp.zeros((1, LANES), F32),
        ],
        axis=0,
    )
    for s in range(carry_ref.shape[0]):
        carry_ref[s] = block


def products_kernel(
    me_ref, carry_ref, g_ref, st_ref, ad_ref, b_ref,
    half_ref, grads_ref, rates_ref, into, back,
):
    devices = carry_ref.shape[0]
    blocks, both, _ = g_ref.shape
    tokens = both // 2
    entering = jnp.zeros((1, LANES), F32)
    for s in range(devices):
        into[s : s + 1, :] = entering
        entering = carry_ref[s, 0:1, :] * entering + carry_ref[s, 1:2, :]
    leaving = jnp.zeros((1, LANES), F32)
    total = jnp.zeros((1, LANES), F32)
    for s in reversed(range(devices)):
        back[s : s + 1, :] = leaving
        here = into[s : s + 1, :]
        total = total + (
            carry_ref[s, 3:4, :]
            + carry_ref[s, 4:5, :] * here
            + leaving * (carry_ref[s, 5:6, :] + carry_ref[s, 6:7, :] * here)
        )
        leaving = carry_ref[s, 0:1, :] * leaving + carry_ref[s, 2:3, :]
    rates_ref[...] = -total
    me = me_ref[0]
    adjoint = (ad_ref[...] + b_ref[REM] * back[pl.ds(me, 1), :]).astype(BF16)
    state = (st_ref[...] + b_ref[CUM] * into[pl.ds(me, 1), :]).astype(BF16)
    half_ref[...] = adjoint
    half = LANES // 2
    for k in range(0, blocks, 2):
        x = jnp.concatenate([g_ref[k, :tokens, :], g_ref[k + 1, :tokens, :]], axis=1)
        y = jnp.concatenate([g_ref[k, tokens:, :], g_ref[k + 1, tokens:, :]], axis=1)
        gi = lax.dot_general(adjoint, x, (((0,), (0,)), ((), ())), preferred_element_type=F32)
        go = lax.dot_general(state, y, (((0,), (0,)), ((), ())), preferred_element_type=F32)
        for q in range(2):
            lanes = slice(q * LANES, (q + 1) * LANES)
            a = gi[:, lanes].astype(BF16)
            b = go[:, lanes].T.astype(BF16)
            for r in range(2):
                rows = slice(r * half, (r + 1) * half)
                grads_ref[2 * (k + q) + r, :half, :] = a[rows]
                grads_ref[2 * (k + q) + r, half:, :] = b[rows]


def sum_kernel(parts_ref, out_ref):
    total = parts_ref[0].astype(F32)
    for s in range(1, parts_ref.shape[0]):
        total = total + parts_ref[s].astype(F32)
    out_ref[...] = total.astype(BF16)


def sum_and_repeat_kernel(parts_ref, out_ref):
    total = parts_ref[0].astype(F32)
    for s in range(1, parts_ref.shape[0]):
        total = total + parts_ref[s].astype(F32)
    total = total.astype(BF16)
    for s in range(out_ref.shape[0]):
        out_ref[s] = total


def repeat_kernel(part_ref, out_ref):
    for s in range(out_ref.shape[0]):
        out_ref[s] = part_ref[...]


def inputs_kernel(half_ref, col_ref, out_ref, done_ref):
    done_ref[...] = jnp.zeros_like(done_ref)
    blocks = half_ref.shape[0]
    a = jnp.concatenate([half_ref[k] for k in range(blocks)], axis=1)
    w = jnp.concatenate(
        [col_ref[y, k] for k in range(blocks) for y in range(col_ref.shape[0])], axis=0
    )
    out_ref[...] = jnp.dot(a, w, preferred_element_type=F32).astype(BF16)


def finish_kernel(parts_ref, done_ref, gi_ref, go_ref):
    half = LANES // 2
    for k in range(parts_ref.shape[0] // 2):
        for r in range(2):
            rows = slice(r * half, (r + 1) * half)
            gi_ref[rows, k * LANES : (k + 1) * LANES] = parts_ref[2 * k + r, :half, :].astype(F32)
            rows = slice(k * LANES + r * half, k * LANES + (r + 1) * half)
            go_ref[rows, :] = parts_ref[2 * k + r, half:, :].astype(F32)


def on_device(inputs, out_grad, in_proj, out_proj, rates, time_step):
    tokens = inputs.shape[0]
    features = in_proj.shape[1]
    blocks = lax.axis_size("state")
    devices = lax.axis_size("seq")
    outer = devices // INNER
    along_y = [[x * INNER + y for y in range(INNER)] for x in range(outer)]
    along_x = [[x * INNER + y for x in range(outer)] for y in range(INNER)]
    sds = jax.ShapeDtypeStruct
    seen = sds((tokens, LANES), F32)
    me = lax.axis_index("seq").astype(jnp.int32).reshape(1)

    def exchange(x, groups):
        return lax.all_to_all(x, "seq", 0, 0, tiled=True, axis_index_groups=groups)

    def parted(shape):
        return [pltpu.VMEM(shape, BF16), pltpu.SemaphoreType.DMA((PARTS,))]

    together = call(
        join_kernel,
        sds((2 * tokens, LANES), BF16),
        in_specs=[HBM] * 2,
        out_specs=HBM,
        scratch=[pltpu.VMEM((2 * tokens, LANES), BF16), pltpu.SemaphoreType.DMA((4,))],
        limit=60 * 1024 * 1024,
    )(inputs, out_grad)
    gathered = lax.all_gather(together, "state", axis=0)
    rows = LANES // INNER
    place = lax.rem(lax.axis_index("seq").astype(jnp.int32), jnp.int32(INNER))
    columns = lax.dynamic_slice_in_dim(in_proj, place * rows, rows, 0)
    columns = jnp.moveaxis(columns.reshape(rows, blocks, LANES), 1, 0)
    columns = lax.all_to_all(columns, "state", 0, 0, tiled=True)
    columns = exchange(jnp.broadcast_to(columns, (INNER, *columns.shape)), along_y)
    following = jnp.concatenate([time_step[1:], jnp.zeros((1,), F32)])
    decays, whole, ends = call(
        decays_kernel,
        (
            sds((KINDS, tokens, LANES), F32),
            sds((2, tokens, LANES), F32),
            sds((2 * ROWS, LANES), F32),
        ),
        in_specs=[VMEM] * 5 + [ANY],
    )(time_step[:, None], following[:, None], rates[None, :], in_proj, out_proj, columns)
    states, adjoints, carry, gathered = call(
        scans_kernel,
        (seen, seen, sds((devices, ROWS, LANES), F32), sds(gathered.shape, BF16)),
        in_specs=[SMEM, HBM] + [VMEM] * 5,
        scratch=[pltpu.VMEM((tokens, LANES), F32)] * 2 + [pltpu.SemaphoreType.DMA((PARTS,))],
        cost=estimate(4 * tokens * features * LANES, 7 << 20),
        limit=SCANS,
    )(me, gathered, in_proj, out_proj, decays, whole, ends)
    carry = exchange(carry, None)
    half, grads, grad_rates = call(
        products_kernel,
        (
            sds((tokens, LANES), BF16),
            sds((devices, features * 2 // devices, LANES), BF16),
            sds((1, LANES), F32),
        ),
        in_specs=[SMEM] + [VMEM] * 5,
        scratch=[pltpu.VMEM((devices, LANES), F32)] * 2,
        cost=estimate(4 * tokens * features * LANES, 7 << 20),
        limit=PRODS,
    )(me, carry, gathered, states, adjoints, whole)
    half_all = lax.all_gather(half, "state", axis=0)
    rows = grads.shape[1]
    part = sds((INNER * rows, LANES), BF16)
    grads = exchange(grads.reshape(outer, INNER * rows, LANES), along_x)
    grads = call(sum_kernel, part)(grads)
    grads = exchange(grads.reshape(INNER, rows, LANES), along_y)
    grads = call(sum_and_repeat_kernel, sds((INNER, rows, LANES), BF16))(grads)
    grads = exchange(grads, along_y)
    grads = call(repeat_kernel, sds((outer, *part.shape), BF16))(grads.reshape(part.shape))
    grads = exchange(grads, along_x).reshape(devices, rows, LANES)
    grad_inputs, done = call(
        inputs_kernel,
        (sds((tokens, LANES), BF16), sds((ROWS, LANES), F32)),
        cost=estimate(2 * tokens * features * LANES, 3 << 20),
    )(half_all, columns)
    grad_in, grad_out = call(
        finish_kernel,
        (sds((LANES, features), F32), sds((features, LANES), F32)),
        in_specs=[VMEM, ANY],
    )(grads, done)
    return grad_inputs, grad_in, grad_out, grad_rates[0]


def solution(mesh):
    placed = (
        P("seq", "state"),
        P("seq", "state"),
        P("state", None),
        P(None, "state"),
        P("state"),
        P("seq"),
    )
    return jax.shard_map(
        on_device,
        mesh=mesh,
        in_specs=placed,
        out_specs=(P("seq", "state"), P("state", None), P(None, "state"), P("state")),
        check_vma=False,
    )
```
